32 devices in a mesh: dp: 8 (over y, x, core), proto: 4 (over z).
Axes of the slice: x: 2, y: 2, z: 4, core: 2. Of those that a mesh axis runs over, the one named last changes fastest.
Arguments:
- features: bfloat16 [4096, 2048], P('dp', 'proto'), may hold values from -8 to 8
- head_weight: bfloat16 [2048, 256], P('proto'), may hold values from -1 to 1
- prototypes: bfloat16 [256, 32768], P(None, 'proto'), may hold values from -1 to 1
Outputs:
- codes: bfloat16 [4096, 32768], P('dp', 'proto')
- proto_grad: float32 [256, 32768], P('dp', 'proto')
- head_grad: float32 [256, 2048], P('dp', 'proto')
The draws below stay inside these ranges and needn't reach their ends.
All inputs are finite; a program needn't handle non-finite values.
Results may differ from the reference program's by a relative error of at most 0.009.
Values may be sent and summed in bfloat16 or wider, within the bound.
A program may use at most 128 MiB of HBM per device.

```python
import jax
import jax.numpy as jnp
from jax import lax

IN = 2048
EMB = 256
PROTOS = 32768
ITERS = 3
TOKENS = 4096


def common_dirs(key):
    key_in = jax.random.fold_in(key, 21)
    key_emb = jax.random.fold_in(key, 22)
    dirs_in = jnp.where(jax.random.bernoulli(key_in, 0.5, (4, IN)), 1.0, -1.0).astype(jnp.float32)
    signs = jnp.where(jax.random.bernoulli(key_emb, 0.5, (EMB,)), 1.0, -1.0).astype(jnp.float32)
    coord = jnp.arange(EMB) // (EMB // 4)
    member = (coord[None, :] == jnp.arange(4)[:, None]).astype(jnp.float32)
    dirs_emb = member * signs[None, :] / jnp.sqrt(jnp.float32(EMB // 4))
    return (dirs_in, dirs_emb)


def draw_features(key, part):
    key_mean = jax.random.fold_in(key, 11)
    key_noise = jax.random.fold_in(key, 12)
    key_group = jax.random.fold_in(key, 14)
    dirs_in, dirs_emb = common_dirs(key)
    group = jax.random.randint(key_group, (TOKENS,), 0, 4)
    shared = 0.5 * jax.random.normal(key_mean, (IN,), jnp.float32)
    values = jax.random.normal(key_noise, (TOKENS, IN), jnp.float32) + 0.8 * dirs_in[group] + shared[None, :]
    return jnp.clip(values, -8.0, 8.0).astype(jnp.bfloat16)


def draw_head_weight(key, part):
    key_noise = jax.random.fold_in(key, 31)
    dirs_in, dirs_emb = common_dirs(key)
    noise = jax.random.normal(key_noise, (IN, EMB), jnp.float32) / jnp.sqrt(jnp.float32(IN))
    coupling = jnp.sqrt(jnp.float32(EMB)) / (0.8 * IN)
    signal = jnp.sum(dirs_in[:, :, None] * dirs_emb[:, None, :], axis=0)
    return jnp.clip(noise + coupling * signal, -1.0, 1.0).astype(jnp.bfloat16)


def draw_prototypes(key, part):
    key_noise = jax.random.fold_in(key, 41)
    dirs_in, dirs_emb = common_dirs(key)
    noise = jax.random.normal(key_noise, (EMB, PROTOS), jnp.float32) / jnp.sqrt(jnp.float32(EMB))
    block = jnp.arange(PROTOS) * 4 // PROTOS
    strength = 0.15 * (block.astype(jnp.float32) + 1.0)
    values = noise + strength[None, :] * dirs_emb[block].T
    return jnp.clip(values, -1.0, 1.0).astype(jnp.bfloat16)


def setup_inputs(seed: int = 0) -> dict:
    key_of = jax.random.split(jax.random.key(seed), 4)
    features = draw_features(jax.random.fold_in(key_of[3], 71), 0)
    head_weight = draw_head_weight(jax.random.fold_in(key_of[3], 71), 0)
    prototypes = draw_prototypes(jax.random.fold_in(key_of[3], 71), 0)
    return dict(features=features, head_weight=head_weight, prototypes=prototypes)


sink_eps = 0.05
soft_temp = 0.1

def reference(features, head_weight, prototypes):
    projected = jnp.dot(features, head_weight, preferred_element_type=jnp.float32)
    length = jnp.sqrt(lax.optimization_barrier(jnp.sum(projected * projected, axis=1, keepdims=True)) + 1e-06)
    unit = projected / length
    unit_b = unit.astype(jnp.bfloat16)
    proto_f = prototypes.astype(jnp.float32)
    normed = (proto_f / jnp.sqrt(lax.optimization_barrier(jnp.sum(proto_f * proto_f, axis=0, keepdims=True)) + 1e-06)).astype(jnp.bfloat16)
    scores = jnp.dot(unit_b, normed, preferred_element_type=jnp.float32)
    col_scale = jnp.ones((PROTOS,), jnp.float32)
    row_scale = jnp.ones((TOKENS,), jnp.float32)
    for step in range(ITERS):
        col_sum = lax.optimization_barrier(jnp.sum(jnp.exp(scores / sink_eps) * col_scale[None, :] * row_scale[:, None], axis=0))
        col_scale = col_scale / col_sum
        row_sum = lax.optimization_barrier(jnp.sum(jnp.exp(scores / sink_eps) * col_scale[None, :] * row_scale[:, None], axis=1))
        row_scale = row_scale / row_sum
    plan = jnp.exp(scores / sink_eps) * col_scale[None, :] * row_scale[:, None]
    soft = jnp.exp(scores / soft_temp)
    probs = soft / lax.optimization_barrier(jnp.sum(soft, axis=1, keepdims=True))
    codes = (PROTOS * plan).astype(jnp.bfloat16)
    factor = PROTOS / (soft_temp * jnp.sqrt(jnp.float32(TOKENS)))
    dscore = ((probs - plan) * factor).astype(jnp.bfloat16)
    proto_grad = lax.dot_general(unit_b, dscore, (((0,), (0,)), ((), ())), preferred_element_type=jnp.float32)
    dunit = lax.dot_general(dscore, normed, (((1,), (1,)), ((), ())), preferred_element_type=jnp.float32)
    dproj = ((dunit - unit * lax.optimization_barrier(jnp.sum(unit * dunit, axis=1, keepdims=True))) / length).astype(jnp.bfloat16)
    head_grad = lax.dot_general(dproj, features, (((0,), (0,)), ((), ())), preferred_element_type=jnp.float32)
    return (codes, proto_grad, head_grad)
```

```python
import functools
import math

import jax
import jax.numpy as jnp
from jax import lax
from jax.experimental import pallas as pl
from jax.experimental.pallas import tpu as pltpu
from jax.sharding import PartitionSpec as P

PROTOS = 32768
ITERS = 3
SOFT_TEMP = 0.1
CHUNKS = 4
F32 = jnp.float32
BF16 = jnp.bfloat16


def kernel(D, Z, f_ref, w_ref, p_ref, codes_ref, pg_ref, hg_ref,
           nb, S, cs, c8, racc, rcol, tcol, psend, precv, ub, ubt, unit_s, len_s,
           colsend, colrecv, rsend, rrecv, cst, dbuf, dacc, dusend, durecv, dpall,
           gsend, garecv, gbrecv,
           psem_s, psem_r, usem_s, usem_r, csem_s, csem_r, rsem_s, rsem_r,
           dsem_s, dsem_r, hsem_s, hsem_r, asem_s, asem_r, bsem_s, bsem_r, osem):
    T, FI = f_ref.shape
    EMB, N = p_ref.shape
    R = T // Z
    H = D // 2
    ROWS = EMB // D
    CW = N // CHUNKS
    md = lax.axis_index("dp")
    mz = lax.axis_index("proto")
    mc = lax.rem(md, 2)
    chip = md // 2
    pc = 1 - mc

    def zpeer(k):
        return lax.rem(mz + k, Z)

    def dpeer(k):
        return lax.rem(md + k, D)

    def remote(src, dst, s, r, **dev):
        return pltpu.make_async_remote_copy(
            src_ref=src, dst_ref=dst, send_sem=s, recv_sem=r,
            device_id=dev, device_id_type=pl.DeviceIdType.MESH)

    barrier = pltpu.get_barrier_semaphore()
    for k in range(1, D):
        pl.semaphore_signal(barrier, inc=1, device_id={"dp": dpeer(k)},
                            device_id_type=pl.DeviceIdType.MESH)
    for k in range(1, Z):
        pl.semaphore_signal(barrier, inc=1, device_id={"proto": zpeer(k)},
                            device_id_type=pl.DeviceIdType.MESH)

    for b in range(Z):
        psend[b] = jnp.dot(f_ref[b * R:(b + 1) * R, :], w_ref[...],
                           preferred_element_type=F32).astype(BF16)
    pl.semaphore_wait(barrier, D + Z - 2)

    sends = []
    pcs = []
    for k in range(1, Z):
        cp = remote(psend.at[zpeer(k)], precv.at[k - 1], psem_s.at[k - 1], psem_r.at[k - 1],
                    proto=zpeer(k))
        cp.start()
        pcs.append(cp)
    sends += pcs

    NB = 256

    @pl.loop(0, N // NB)
    def _(j):
        cols = pl.ds(pl.multiple_of(j * NB, NB), NB)
        sq = jnp.zeros((8, NB), F32)
        for g in range(EMB // 32):
            x = p_ref[g * 32:(g + 1) * 32, cols].astype(F32)
            x = x * x
            sq = sq + ((x[0:8] + x[8:16]) + (x[16:24] + x[24:32]))
        inv = 1.0 / jnp.sqrt(jnp.sum(sq, axis=0, keepdims=True) + 1e-06)
        for g in range(EMB // 32):
            x = p_ref[g * 32:(g + 1) * 32, cols].astype(F32)
            nb[g * 32:(g + 1) * 32, cols] = (x * inv).astype(BF16)
        cs[:, cols] = jnp.zeros((8, NB), F32)

    myrows = pl.ds(pl.multiple_of(mz * R, R), R)
    proj = jnp.dot(f_ref[myrows, :], w_ref[...], preferred_element_type=F32)
    for cp in pcs:
        cp.wait_recv()
    for k in range(1, Z):
        proj = proj + precv[k - 1].astype(F32)
    length = jnp.sqrt(jnp.sum(proj * proj, axis=1, keepdims=True) + 1e-06)
    unit = proj / length
    unit_s[...] = unit
    len_s[...] = jnp.broadcast_to(length, (R, 128))
    ub[myrows, :] = unit.astype(BF16)
    ucs = []
    for k in range(1, Z):
        cp = remote(ub.at[myrows, :], ub.at[myrows, :], usem_s.at[k - 1], usem_r.at[k - 1],
                    proto=zpeer(k))
        cp.start()
        ucs.append(cp)
    sends += ucs

    SB = 512

    def score_rows(z):
        rows = pl.ds(pl.multiple_of(z * R, R), R)
        u = ub[rows, :]

        def body(j, acc):
            cols = pl.ds(pl.multiple_of(j * SB, SB), SB)
            s = jnp.dot(u, nb[:, cols], preferred_element_type=F32)
            e = jnp.exp(s * (1.0 / SOFT_TEMP))
            S[rows, cols] = e
            e2 = e * e
            cs[:, cols] += jnp.sum(e2.reshape(R // 8, 8, SB), axis=0)
            for i in range(SB // 128):
                acc = acc + e[:, i * 128:(i + 1) * 128]
            return acc

        racc[rows, :] = lax.fori_loop(0, N // SB, body, jnp.zeros((R, 128), F32))

    for k in range(Z):
        if k:
            ucs[k - 1].wait_recv()
        score_rows(lax.rem(mz + Z - k, Z))

    def start_rows(it):
        v = jnp.sum(jnp.transpose(racc[...]), axis=0, keepdims=True)
        rsend[it] = v
        out = []
        for k in range(1, Z):
            cp = remote(rsend.at[it], rrecv.at[it, k - 1], rsem_s.at[it, k - 1],
                        rsem_r.at[it, k - 1], proto=zpeer(k))
            cp.start()
            out.append(cp)
        return out

    def end_rows(it, cps):
        for cp in cps:
            cp.wait_recv()
        v = rsend[it]
        for k in range(1, Z):
            v = v + rrecv[it, k - 1]
        return 1.0 / v

    def to_col(v):
        return jnp.transpose(jnp.broadcast_to(v, (128, T)))

    def start_cols(it):
        colsend[it] = jnp.sum(cs[...], axis=0, keepdims=True)
        out = []
        for k in range(1, D):
            cp = remote(colsend.at[it], colrecv.at[it, k - 1], csem_s.at[it, k - 1],
                        csem_r.at[it, k - 1], dp=dpeer(k))
            cp.start()
            out.append(cp)
        return out

    def end_cols(it, cps):
        for cp in cps:
            cp.wait_recv()
        v = colsend[it]
        for k in range(1, D):
            v = v + colrecv[it, k - 1]
        c8[...] = jnp.broadcast_to(1.0 / v, (8, N))

    def row_pass():
        G = 64

        @pl.loop(0, T // G)
        def _(g):
            rows = pl.ds(pl.multiple_of(g * G, G), G)

            def body(j, acc):
                for i in range(8):
                    cols = pl.ds(pl.multiple_of(j * 1024 + i * 128, 128), 128)
                    c = c8[:, cols]
                    new = []
                    for q in range(G // 8):
                        x = S[pl.ds(pl.multiple_of(g * G + q * 8, 8), 8), cols]
                        new.append(acc[q] + x * x * c)
                    acc = tuple(new)
                return acc

            acc = lax.fori_loop(0, N // 1024, body,
                                tuple(jnp.zeros((8, 128), F32) for _ in range(G // 8)))
            racc[rows, :] = jnp.concatenate(acc, axis=0)

    def col_pass():
        W = 1024

        @pl.loop(0, N // W)
        def _(j):
            def body(g, acc):
                for q in range(8):
                    rows = pl.ds(pl.multiple_of(g * 64 + q * 8, 8), 8)
                    r = rcol[rows, :]
                    new = []
                    for i in range(W // 128):
                        x = S[rows, pl.ds(pl.multiple_of(j * W + i * 128, 128), 128)]
                        new.append(acc[i] + x * x * r)
                    acc = tuple(new)
                return acc

            acc = lax.fori_loop(0, T // 64, body,
                                tuple(jnp.zeros((8, 128), F32) for _ in range(W // 128)))
            cs[:, pl.ds(pl.multiple_of(j * W, W), W)] = jnp.concatenate(acc, axis=1)

    soft_cps = None
    kf = 1.0 / (SOFT_TEMP * math.sqrt(D * T))
    for it in range(ITERS):
        cps = start_cols(it)
        sends += cps
        if it == 0:
            soft_cps = start_rows(ITERS)
            sends += soft_cps
            ubt[...] = jnp.transpose(ub[...].astype(F32)).astype(BF16)
        end_cols(it, cps)
        row_pass()
        cps = start_rows(it)
        sends += cps
        if it == 0:
            tcol[...] = to_col(end_rows(ITERS, soft_cps) * (PROTOS * kf))
        inv = end_rows(it, cps)
        if it < ITERS - 1:
            rcol[...] = to_col(inv)
            col_pass()
        else:
            rcol[...] = to_col(inv * PROTOS)

    FB = 256
    dacc[...] = jnp.zeros_like(dacc)

    def chunk_cols(q):
        return (pl.ds(q * CW, CW) if q < CHUNKS else pl.ds(N, FI))

    def start_a(q):
        cols = chunk_cols(q)
        cp = remote(gsend.at[pl.ds(pc * H, H), :, cols], garecv.at[:, :, cols],
                    asem_s.at[q], asem_r.at[q], dp=md + 1 - 2 * mc)
        cp.start()
        sends.append(cp)
        return cp

    def start_b(q, cpa):
        cpa.wait_recv()
        cols = chunk_cols(q)

        @pl.loop(0, H)
        def _(k):
            gsend[mc * H + k, :, cols] = (gsend[mc * H + k, :, cols].astype(F32)
                                          + garecv[k, :, cols].astype(F32)).astype(BF16)

        out = []
        for k in range(1, H):
            dst = lax.rem(chip + k, H)
            cp = remote(gsend.at[mc * H + dst, :, cols], gbrecv.at[k - 1, :, cols],
                        bsem_s.at[q, k - 1], bsem_r.at[q, k - 1], dp=dst * 2 + mc)
            cp.start()
            out.append(cp)
        sends.extend(out)
        return out

    def finish(q, cps):
        for cp in cps:
            cp.wait_recv()
        cols = chunk_cols(q)
        v = gsend[mc * H + chip, :, cols].astype(F32)
        for k in range(1, H):
            v = v + gbrecv[k - 1, :, cols].astype(F32)
        if q < CHUNKS:
            pg_ref[:, cols] = v
        else:
            hg_ref[...] = v

    outs = []
    acp = []
    bcp = []
    for q in range(CHUNKS):
        slot = q % 2
        if q >= 2:
            outs[q - 2].wait()

        @pl.loop(0, CW // FB)
        def _(j, q=q, slot=slot):
            lcols = pl.ds(pl.multiple_of(j * FB, FB), FB)
            cols = pl.ds(pl.multiple_of(q * CW + j * FB, FB), FB)
            c = c8[:, cols][0:1, :]

            @pl.loop(0, T // 32)
            def _(g):
                rows = pl.ds(pl.multiple_of(g * 32, 32), 32)
                x = S[rows, cols]
                r = rcol[rows, :]
                t = tcol[rows, :]
                r = jnp.concatenate([r] * (FB // 128), axis=1)
                t = jnp.concatenate([t] * (FB // 128), axis=1)
                plan = x * x * c * r
                cst[slot, rows, lcols] = plan.astype(BF16)
                dbuf[rows, :] = (x * t - plan * kf).astype(BF16)

            d = dbuf[...]
            dacc[...] += lax.dot_general(d, nb[:, cols], (((1,), (1,)), ((), ())),
                                         preferred_element_type=F32)
            res = jnp.dot(ubt[...], d, preferred_element_type=F32).astype(BF16)
            for e in range(D):
                gsend[(e % 2) * H + e // 2, :, cols] = res[e * ROWS:(e + 1) * ROWS, :]

        cp = pltpu.make_async_copy(cst.at[slot], codes_ref.at[:, pl.ds(q * CW, CW)], osem.at[q])
        cp.start()
        outs.append(cp)
        acp.append(start_a(q))
        if q == CHUNKS - 1:
            for b in range(Z):
                dusend[b] = dacc[b * R:(b + 1) * R, :].astype(BF16)
            dcs = []
            for k in range(1, Z):
                cp = remote(dusend.at[zpeer(k)], durecv.at[k - 1], dsem_s.at[k - 1],
                            dsem_r.at[k - 1], proto=zpeer(k))
                cp.start()
                dcs.append(cp)
            sends += dcs
        if q >= 1:
            bcp.append(start_b(q - 1, acp[q - 1]))

    du = dacc[myrows, :]
    for cp in dcs:
        cp.wait_recv()
    for k in range(1, Z):
        du = du + durecv[k - 1].astype(F32)
    unit = unit_s[...]
    dp = (du - unit * jnp.sum(unit * du, axis=1, keepdims=True)) / len_s[:, 0:1]
    dpall[myrows, :] = dp.astype(BF16)
    hcs = []
    for k in range(1, Z):
        cp = remote(dpall.at[myrows, :], dpall.at[myrows, :], hsem_s.at[k - 1], hsem_r.at[k - 1],
                    proto=zpeer(k))
        cp.start()
        hcs.append(cp)
    sends += hcs
    bcp.append(start_b(CHUNKS - 1, acp[CHUNKS - 1]))
    for cp in hcs:
        cp.wait_recv()
    dpt = jnp.transpose(dpall[...].astype(F32)).astype(BF16)
    res = jnp.dot(dpt, f_ref[...], preferred_element_type=F32).astype(BF16)
    for e in range(D):
        gsend[(e % 2) * H + e // 2, :, N:N + FI] = res[e * ROWS:(e + 1) * ROWS, :]
    acp.append(start_a(CHUNKS))
    bcp.append(start_b(CHUNKS, acp[CHUNKS]))
    for q in range(CHUNKS + 1):
        finish(q, bcp[q])
    for cp in outs[-2:]:
        cp.wait()
    for cp in sends:
        cp.wait_send()


def solution(mesh):
    D, Z = mesh.shape["dp"], mesh.shape["proto"]

    def on_device(features, head_weight, prototypes):
        T, FI = features.shape
        EMB, N = prototypes.shape
        R, H, ROWS, C = T // Z, D // 2, EMB // D, N + FI
        V = pltpu.VMEM
        dma = pltpu.SemaphoreType.DMA
        vspec = pl.BlockSpec(memory_space=pltpu.VMEM)
        return pl.pallas_call(
            functools.partial(kernel, D, Z),
            out_shape=(
                jax.ShapeDtypeStruct((T, N), BF16),
                jax.ShapeDtypeStruct((ROWS, N), F32),
                jax.ShapeDtypeStruct((ROWS, FI), F32),
            ),
            in_specs=[vspec] * 3,
            out_specs=(pl.BlockSpec(memory_space=pl.ANY), vspec, vspec),
            scratch_shapes=[
                V((EMB, N), BF16), V((T, N), F32), V((8, N), F32), V((8, N), F32),
                V((T, 128), F32), V((T, 128), F32), V((T, 128), F32),
                V((Z, R, EMB), BF16), V((Z - 1, R, EMB), BF16),
                V((T, EMB), BF16), V((EMB, T), BF16), V((R, EMB), F32), V((R, 128), F32),
                V((ITERS, 1, N), F32), V((ITERS, D - 1, 1, N), F32),
                V((ITERS + 1, 1, T), F32), V((ITERS + 1, Z - 1, 1, T), F32),
                V((2, T, N // CHUNKS), BF16), V((T, 256), BF16), V((T, EMB), F32),
                V((Z, R, EMB), BF16), V((Z - 1, R, EMB), BF16), V((T, EMB), BF16),
                V((D, ROWS, C), BF16), V((H, ROWS, C), BF16), V((H - 1, ROWS, C), BF16),
                dma((Z - 1,)), dma((Z - 1,)), dma((Z - 1,)), dma((Z - 1,)),
                dma((ITERS, D - 1)), dma((ITERS, D - 1)),
                dma((ITERS + 1, Z - 1)), dma((ITERS + 1, Z - 1)),
                dma((Z - 1,)), dma((Z - 1,)), dma((Z - 1,)), dma((Z - 1,)),
                dma((CHUNKS + 1,)), dma((CHUNKS + 1,)),
                dma((CHUNKS + 1, H - 1)), dma((CHUNKS + 1, H - 1)),
                dma((CHUNKS,)),
            ],
            compiler_params=pltpu.CompilerParams(
                collective_id=0, has_side_effects=True, vmem_limit_bytes=60 * 1024 * 1024),
            cost_estimate=pl.CostEstimate(
                flops=6 * T * N * EMB, bytes_accessed=16 * 1024 * 1024,
                transcendentals=T * N),
        )(features, head_weight, prototypes)

    return jax.shard_map(
        on_device, mesh=mesh,
        in_specs=(P("dp", "proto"), P("proto", None), P(None, "proto")),
        out_specs=(P("dp", "proto"), P("dp", "proto"), P("dp", "proto")),
        check_vma=False)
```

```python
import functools
import math

import jax
import jax.numpy as jnp
from jax import lax
from jax.experimental import pallas as pl
from jax.experimental.pallas import tpu as pltpu
from jax.sharding import PartitionSpec as P

PROTOS = 32768
ITERS = 3
SOFT_TEMP = 0.1
CHUNKS = 4
F32 = jnp.float32
BF16 = jnp.bfloat16


def kernel(D, Z, f_ref, w_ref, p_ref, codes_ref, pg_ref, hg_ref,
           nb, S, cs, c8, racc, rcol, tcol, psend, precv, ub, ubt, unit_s, len_s,
           colsend, colrecv, rsend, rrecv, cst, dbuf, dacc, dusend, durecv, dpall,
           gsend, garecv, gbrecv,
           psem_s, psem_r, usem_s, usem_r, csem_s, csem_r, rsem_s, rsem_r,
           dsem_s, dsem_r, hsem_s, hsem_r, asem_s, asem_r, bsem_s, bsem_r, osem):
    T, FI = f_ref.shape
    EMB, N = p_ref.shape
    R = T // Z
    H = D // 2
    ROWS = EMB // D
    CW = N // CHUNKS
    md = lax.axis_index("dp")
    mz = lax.axis_index("proto")
    mc = lax.rem(md, 2)
    chip = md // 2
    pc = 1 - mc

    def zpeer(k):
        return lax.rem(mz + k, Z)

    def dpeer(k):
        return lax.rem(md + k, D)

    def remote(src, dst, s, r, **dev):
        return pltpu.make_async_remote_copy(
            src_ref=src, dst_ref=dst, send_sem=s, recv_sem=r,
            device_id=dev, device_id_type=pl.DeviceIdType.MESH)

    barrier = pltpu.get_barrier_semaphore()
    for k in range(1, D):
        pl.semaphore_signal(barrier, inc=1, device_id={"dp": dpeer(k)},
                            device_id_type=pl.DeviceIdType.MESH)
    for k in range(1, Z):
        pl.semaphore_signal(barrier, inc=1, device_id={"proto": zpeer(k)},
                            device_id_type=pl.DeviceIdType.MESH)

    for b in range(Z):
        psend[b] = jnp.dot(f_ref[b * R:(b + 1) * R, :], w_ref[...],
                           preferred_element_type=F32).astype(BF16)
    pl.semaphore_wait(barrier, D + Z - 2)

    sends = []
    pcs = []
    for k in range(1, Z):
        cp = remote(psend.at[zpeer(k)], precv.at[k - 1], psem_s.at[k - 1], psem_r.at[k - 1],
                    proto=zpeer(k))
        cp.start()
        pcs.append(cp)
    sends += pcs

    NB = 256

    @pl.loop(0, N // NB)
    def _(j):
        cols = pl.ds(pl.multiple_of(j * NB, NB), NB)
        sq = jnp.zeros((8, NB), F32)
        for g in range(EMB // 32):
            x = p_ref[g * 32:(g + 1) * 32, cols].astype(F32)
            x = x * x
            sq = sq + ((x[0:8] + x[8:16]) + (x[16:24] + x[24:32]))
        inv = 1.0 / jnp.sqrt(jnp.sum(sq, axis=0, keepdims=True) + 1e-06)
        for g in range(EMB // 32):
            x = p_ref[g * 32:(g + 1) * 32, cols].astype(F32)
            nb[g * 32:(g + 1) * 32, cols] = (x * inv).astype(BF16)
        cs[:, cols] = jnp.zeros((8, NB), F32)

    myrows = pl.ds(pl.multiple_of(mz * R, R), R)
    proj = jnp.dot(f_ref[myrows, :], w_ref[...], preferred_element_type=F32)
    for cp in pcs:
        cp.wait_recv()
    for k in range(1, Z):
        proj = proj + precv[k - 1].astype(F32)
    length = jnp.sqrt(jnp.sum(proj * proj, axis=1, keepdims=True) + 1e-06)
    unit = proj / length
    unit_s[...] = unit
    len_s[...] = jnp.broadcast_to(length, (R, 128))
    ub[myrows, :] = unit.astype(BF16)
    ucs = []
    for k in range(1, Z):
        cp = remote(ub.at[myrows, :], ub.at[myrows, :], usem_s.at[k - 1], usem_r.at[k - 1],
                    proto=zpeer(k))
        cp.start()
        ucs.append(cp)
    sends += ucs

    SB = 512

    def score_rows(z):
        rows = pl.ds(pl.multiple_of(z * R, R), R)
        u = ub[rows, :]

        def body(j, acc):
            cols = pl.ds(pl.multiple_of(j * SB, SB), SB)
            s = jnp.dot(u, nb[:, cols], preferred_element_type=F32)
            e = jnp.exp2(s * (math.log2(math.e) / SOFT_TEMP))
            S[rows, cols] = e
            e2 = e * e
            cs[:, cols] += jnp.sum(e2.reshape(R // 8, 8, SB), axis=0)
            for i in range(SB // 128):
                acc = acc + e[:, i * 128:(i + 1) * 128]
            return acc

        racc[rows, :] = lax.fori_loop(0, N // SB, body, jnp.zeros((R, 128), F32))

    for k in range(Z):
        if k:
            ucs[k - 1].wait_recv()
        score_rows(lax.rem(mz + Z - k, Z))

    def start_rows(it):
        v = jnp.sum(jnp.transpose(racc[...]), axis=0, keepdims=True)
        rsend[it] = v
        out = []
        for k in range(1, Z):
            cp = remote(rsend.at[it], rrecv.at[it, k - 1], rsem_s.at[it, k - 1],
                        rsem_r.at[it, k - 1], proto=zpeer(k))
            cp.start()
            out.append(cp)
        return out

    def end_rows(it, cps):
        for cp in cps:
            cp.wait_recv()
        v = rsend[it]
        for k in range(1, Z):
            v = v + rrecv[it, k - 1]
        return 1.0 / v

    def to_col(v):
        return jnp.transpose(jnp.broadcast_to(v, (128, T)))

    def start_cols(it):
        v = jnp.sum(cs[...], axis=0, keepdims=True)
        CN = N // 16
        colsend[it] = jnp.concatenate([v[:, i * CN:(i + 1) * CN] for i in range(16)],
                                      axis=0).astype(BF16)
        out = []
        for k in range(1, D):
            cp = remote(colsend.at[it], colrecv.at[it, k - 1], csem_s.at[it, k - 1],
                        csem_r.at[it, k - 1], dp=dpeer(k))
            cp.start()
            out.append(cp)
        return out

    def end_cols(it, cps):
        for cp in cps:
            cp.wait_recv()
        v = colsend[it].astype(F32)
        for k in range(1, D):
            v = v + colrecv[it, k - 1].astype(F32)
        v = 1.0 / v
        CN = N // 16
        for i in range(16):
            c8[:, i * CN:(i + 1) * CN] = jnp.broadcast_to(v[i:i + 1, :], (8, CN))

    def row_pass():
        G = 64

        @pl.loop(0, T // G)
        def _(g):
            rows = pl.ds(pl.multiple_of(g * G, G), G)

            def body(j, acc):
                cols = pl.ds(pl.multiple_of(j * 1024, 1024), 1024)
                blk = S.at[rows, cols]
                cblk = c8.at[:, cols]
                for i in range(8):
                    c = cblk[:, i * 128:(i + 1) * 128]
                    new = []
                    for q in range(G // 8):
                        x = blk[q * 8:(q + 1) * 8, i * 128:(i + 1) * 128]
                        new.append(acc[q] + x * x * c)
                    acc = tuple(new)
                return acc

            acc = lax.fori_loop(0, N // 1024, body,
                                tuple(jnp.zeros((8, 128), F32) for _ in range(G // 8)))
            racc[rows, :] = jnp.concatenate(acc, axis=0)

    def col_pass():
        W = 1024

        @pl.loop(0, N // W)
        def _(j):
            def body(g, acc):
                rows = pl.ds(pl.multiple_of(g * 64, 64), 64)
                blk = S.at[rows, pl.ds(pl.multiple_of(j * W, W), W)]
                rblk = rcol.at[rows, :]
                for q in range(8):
                    r = rblk[q * 8:(q + 1) * 8, :]
                    new = []
                    for i in range(W // 128):
                        x = blk[q * 8:(q + 1) * 8, i * 128:(i + 1) * 128]
                        new.append(acc[i] + x * x * r)
                    acc = tuple(new)
                return acc

            acc = lax.fori_loop(0, T // 64, body,
                                tuple(jnp.zeros((8, 128), F32) for _ in range(W // 128)))
            cs[:, pl.ds(pl.multiple_of(j * W, W), W)] = jnp.concatenate(acc, axis=1)

    soft_cps = None
    kf = 1.0 / (SOFT_TEMP * math.sqrt(D * T))
    for it in range(ITERS):
        cps = start_cols(it)
        sends += cps
        if it == 0:
            soft_cps = start_rows(ITERS)
            sends += soft_cps
            ubt[...] = jnp.transpose(ub[...].astype(F32)).astype(BF16)
        end_cols(it, cps)
        row_pass()
        cps = start_rows(it)
        sends += cps
        if it == 0:
            tcol[...] = to_col(end_rows(ITERS, soft_cps) * (PROTOS * kf))
        inv = end_rows(it, cps)
        if it < ITERS - 1:
            rcol[...] = to_col(inv)
            col_pass()
        else:
            rcol[...] = to_col(inv * PROTOS)

    FB = 512
    dacc[...] = jnp.zeros_like(dacc)

    def chunk_cols(q):
        return (pl.ds(q * CW, CW) if q < CHUNKS else pl.ds(N, FI))

    def start_a(q):
        cols = chunk_cols(q)
        cp = remote(gsend.at[pl.ds(pc * H, H), :, cols], garecv.at[:, :, cols],
                    asem_s.at[q], asem_r.at[q], dp=md + 1 - 2 * mc)
        cp.start()
        sends.append(cp)
        return cp

    def start_b(q, cpa):
        cpa.wait_recv()
        cols = chunk_cols(q)

        @pl.loop(0, H)
        def _(k):
            gsend[mc * H + k, :, cols] = (gsend[mc * H + k, :, cols].astype(F32)
                                          + garecv[k, :, cols].astype(F32)).astype(BF16)

        out = []
        for k in range(1, H):
            dst = lax.rem(chip + k, H)
            cp = remote(gsend.at[mc * H + dst, :, cols], gbrecv.at[k - 1, :, cols],
                        bsem_s.at[q, k - 1], bsem_r.at[q, k - 1], dp=dst * 2 + mc)
            cp.start()
            out.append(cp)
        sends.extend(out)
        return out

    def finish(q, cps):
        for cp in cps:
            cp.wait_recv()
        cols = chunk_cols(q)
        v = gsend[mc * H + chip, :, cols].astype(F32)
        for k in range(1, H):
            v = v + gbrecv[k - 1, :, cols].astype(F32)
        if q < CHUNKS:
            pg_ref[:, cols] = v
        else:
            hg_ref[...] = v

    outs = []
    acp = []
    bcp = []
    for q in range(CHUNKS):
        slot = q % 2
        if q >= 2:
            outs[q - 2].wait()

        @pl.loop(0, CW // FB)
        def _(j, q=q, slot=slot):
            lcols = pl.ds(pl.multiple_of(j * FB, FB), FB)
            cols = pl.ds(pl.multiple_of(q * CW + j * FB, FB), FB)
            c = c8[:, cols][0:1, :]

            @pl.loop(0, T // 32)
            def _(g):
                rows = pl.ds(pl.multiple_of(g * 32, 32), 32)
                xv = S.at[rows, cols]
                rv = rcol.at[rows, :]
                tv = tcol.at[rows, :]
                ov = cst.at[slot, rows, lcols]
                dv = dbuf.at[rows, :]
                for h in range(2):
                    hr = slice(h * 16, h * 16 + 16)
                    r = rv[hr, :]
                    t = tv[hr, :]
                    for i in range(FB // 128):
                        hc = slice(i * 128, i * 128 + 128)
                        x = xv[hr, hc]
                        plan = x * x * c[:, hc] * r
                        ov[hr, hc] = plan.astype(BF16)
                        dv[hr, hc] = (x * t - plan * kf).astype(BF16)

            d = dbuf[...]
            dacc[...] += lax.dot_general(d, nb[:, cols], (((1,), (1,)), ((), ())),
                                         preferred_element_type=F32)
            res = jnp.dot(ubt[...], d, preferred_element_type=F32).astype(BF16)
            for e in range(D):
                gsend[(e % 2) * H + e // 2, :, cols] = res[e * ROWS:(e + 1) * ROWS, :]

        cp = pltpu.make_async_copy(cst.at[slot], codes_ref.at[:, pl.ds(q * CW, CW)], osem.at[q])
        cp.start()
        outs.append(cp)
        acp.append(start_a(q))
        if q == CHUNKS - 1:
            for b in range(Z):
                dusend[b] = dacc[b * R:(b + 1) * R, :].astype(BF16)
            dcs = []
            for k in range(1, Z):
                cp = remote(dusend.at[zpeer(k)], durecv.at[k - 1], dsem_s.at[k - 1],
                            dsem_r.at[k - 1], proto=zpeer(k))
                cp.start()
                dcs.append(cp)
            sends += dcs
        if q >= 1:
            bcp.append(start_b(q - 1, acp[q - 1]))

    du = dacc[myrows, :]
    for cp in dcs:
        cp.wait_recv()
    for k in range(1, Z):
        du = du + durecv[k - 1].astype(F32)
    unit = unit_s[...]
    dp = (du - unit * jnp.sum(unit * du, axis=1, keepdims=True)) / len_s[:, 0:1]
    dpall[myrows, :] = dp.astype(BF16)
    hcs = []
    for k in range(1, Z):
        cp = remote(dpall.at[myrows, :], dpall.at[myrows, :], hsem_s.at[k - 1], hsem_r.at[k - 1],
                    proto=zpeer(k))
        cp.start()
        hcs.append(cp)
    sends += hcs
    bcp.append(start_b(CHUNKS - 1, acp[CHUNKS - 1]))
    for cp in hcs:
        cp.wait_recv()
    dpt = jnp.transpose(dpall[...].astype(F32)).astype(BF16)
    res = jnp.dot(dpt, f_ref[...], preferred_element_type=F32).astype(BF16)
    for e in range(D):
        gsend[(e % 2) * H + e // 2, :, N:N + FI] = res[e * ROWS:(e + 1) * ROWS, :]
    acp.append(start_a(CHUNKS))
    bcp.append(start_b(CHUNKS, acp[CHUNKS]))
    for q in range(CHUNKS + 1):
        finish(q, bcp[q])
    for cp in outs[-2:]:
        cp.wait()
    for cp in sends:
        cp.wait_send()


def solution(mesh):
    D, Z = mesh.shape["dp"], mesh.shape["proto"]

    def on_device(features, head_weight, prototypes):
        T, FI = features.shape
        EMB, N = prototypes.shape
        R, H, ROWS, C = T // Z, D // 2, EMB // D, N + FI
        V = pltpu.VMEM
        dma = pltpu.SemaphoreType.DMA
        vspec = pl.BlockSpec(memory_space=pltpu.VMEM)
        return pl.pallas_call(
            functools.partial(kernel, D, Z),
            out_shape=(
                jax.ShapeDtypeStruct((T, N), BF16),
                jax.ShapeDtypeStruct((ROWS, N), F32),
                jax.ShapeDtypeStruct((ROWS, FI), F32),
            ),
            in_specs=[vspec] * 3,
            out_specs=(pl.BlockSpec(memory_space=pl.ANY), vspec, vspec),
            scratch_shapes=[
                V((EMB, N), BF16), V((T, N), F32), V((8, N), F32), V((8, N), F32),
                V((T, 128), F32), V((T, 128), F32), V((T, 128), F32),
                V((Z, R, EMB), BF16), V((Z - 1, R, EMB), BF16),
                V((T, EMB), BF16), V((EMB, T), BF16), V((R, EMB), F32), V((R, 128), F32),
                V((ITERS, 16, N // 16), BF16), V((ITERS, D - 1, 16, N // 16), BF16),
                V((ITERS + 1, 1, T), F32), V((ITERS + 1, Z - 1, 1, T), F32),
                V((2, T, N // CHUNKS), BF16), V((T, 512), BF16), V((T, EMB), F32),
                V((Z, R, EMB), BF16), V((Z - 1, R, EMB), BF16), V((T, EMB), BF16),
                V((D, ROWS, C), BF16), V((H, ROWS, C), BF16), V((H - 1, ROWS, C), BF16),
                dma((Z - 1,)), dma((Z - 1,)), dma((Z - 1,)), dma((Z - 1,)),
                dma((ITERS, D - 1)), dma((ITERS, D - 1)),
                dma((ITERS + 1, Z - 1)), dma((ITERS + 1, Z - 1)),
                dma((Z - 1,)), dma((Z - 1,)), dma((Z - 1,)), dma((Z - 1,)),
                dma((CHUNKS + 1,)), dma((CHUNKS + 1,)),
                dma((CHUNKS + 1, H - 1)), dma((CHUNKS + 1, H - 1)),
                dma((CHUNKS,)),
            ],
            compiler_params=pltpu.CompilerParams(
                collective_id=0, has_side_effects=True, vmem_limit_bytes=60 * 1024 * 1024),
            cost_estimate=pl.CostEstimate(
                flops=6 * T * N * EMB, bytes_accessed=16 * 1024 * 1024,
                transcendentals=T * N),
        )(features, head_weight, prototypes)

    return jax.shard_map(
        on_device, mesh=mesh,
        in_specs=(P("dp", "proto"), P("proto", None), P(None, "proto")),
        out_specs=(P("dp", "proto"), P("dp", "proto"), P("dp", "proto")),
        check_vma=False)
```

```python
import functools
import math

import jax
import jax.numpy as jnp
from jax import lax
from jax.experimental import pallas as pl
from jax.experimental.pallas import tpu as pltpu
from jax.sharding import PartitionSpec as P

PROTOS = 32768
ITERS = 3
SOFT_TEMP = 0.1
CHUNKS = 4
F32 = jnp.float32
BF16 = jnp.bfloat16


def kernel(D, Z, f_ref, w_ref, p_ref, codes_ref, pg_ref, hg_ref,
           nb, S, cs, c8, racc, rcol, tcol, psend, precv, ub, ubt, unit_s, len_s,
           colsend, colrecv, rsend, rrecv, cst, dbuf, dacc, dusend, durecv, dpall,
           gsend, garecv, gbrecv,
           psem_s, psem_r, usem_s, usem_r, csem_s, csem_r, rsem_s, rsem_r,
           dsem_s, dsem_r, hsem_s, hsem_r, asem_s, asem_r, bsem_s, bsem_r, osem):
    T, FI = f_ref.shape
    EMB, N = p_ref.shape
    R = T // Z
    H = D // 2
    ROWS = EMB // D
    CW = N // CHUNKS
    md = lax.axis_index("dp")
    mz = lax.axis_index("proto")
    mc = lax.rem(md, 2)
    chip = md // 2
    pc = 1 - mc

    def zpeer(k):
        return lax.rem(mz + k, Z)

    def dpeer(k):
        return lax.rem(md + k, D)

    def remote(src, dst, s, r, **dev):
        return pltpu.make_async_remote_copy(
            src_ref=src, dst_ref=dst, send_sem=s, recv_sem=r,
            device_id=dev, device_id_type=pl.DeviceIdType.MESH)

    barrier = pltpu.get_barrier_semaphore()
    for k in range(1, D):
        pl.semaphore_signal(barrier, inc=1, device_id={"dp": dpeer(k)},
                            device_id_type=pl.DeviceIdType.MESH)
    for k in range(1, Z):
        pl.semaphore_signal(barrier, inc=1, device_id={"proto": zpeer(k)},
                            device_id_type=pl.DeviceIdType.MESH)

    for b in range(Z):
        psend[b] = jnp.dot(f_ref[b * R:(b + 1) * R, :], w_ref[...],
                           preferred_element_type=F32).astype(BF16)
    pl.semaphore_wait(barrier, D + Z - 2)

    sends = []
    pcs = []
    for k in range(1, Z):
        cp = remote(psend.at[zpeer(k)], precv.at[k - 1], psem_s.at[k - 1], psem_r.at[k - 1],
                    proto=zpeer(k))
        cp.start()
        pcs.append(cp)
    sends += pcs

    NB = 256

    @pl.loop(0, N // NB)
    def _(j):
        cols = pl.ds(pl.multiple_of(j * NB, NB), NB)
        sq = jnp.zeros((8, NB), F32)
        for g in range(EMB // 32):
            x = p_ref[g * 32:(g + 1) * 32, cols].astype(F32)
            x = x * x
            sq = sq + ((x[0:8] + x[8:16]) + (x[16:24] + x[24:32]))
        inv = 1.0 / jnp.sqrt(jnp.sum(sq, axis=0, keepdims=True) + 1e-06)
        for g in range(EMB // 32):
            x = p_ref[g * 32:(g + 1) * 32, cols].astype(F32)
            nb[g * 32:(g + 1) * 32, cols] = (x * inv).astype(BF16)
        cs[:, cols] = jnp.zeros((8, NB), F32)

    myrows = pl.ds(pl.multiple_of(mz * R, R), R)
    proj = jnp.dot(f_ref[myrows, :], w_ref[...], preferred_element_type=F32)
    for cp in pcs:
        cp.wait_recv()
    for k in range(1, Z):
        proj = proj + precv[k - 1].astype(F32)
    length = jnp.sqrt(jnp.sum(proj * proj, axis=1, keepdims=True) + 1e-06)
    unit = proj / length
    unit_s[...] = unit
    len_s[...] = jnp.broadcast_to(length, (R, 128))
    ub[myrows, :] = unit.astype(BF16)
    ucs = []
    for k in range(1, Z):
        cp = remote(ub.at[myrows, :], ub.at[myrows, :], usem_s.at[k - 1], usem_r.at[k - 1],
                    proto=zpeer(k))
        cp.start()
        ucs.append(cp)
    sends += ucs

    SB = 512

    def score_rows(z):
        rows = pl.ds(pl.multiple_of(z * R, R), R)
        u = ub[rows, :]

        def body(j, acc):
            cols = pl.ds(pl.multiple_of(j * SB, SB), SB)
            s = jnp.dot(u, nb[:, cols], preferred_element_type=F32)
            e = jnp.exp2(s * (math.log2(math.e) / SOFT_TEMP))
            S[rows, cols] = e
            e2 = e * e
            cs[:, cols] += jnp.sum(e2.reshape(R // 8, 8, SB), axis=0)
            for i in range(SB // 128):
                acc = acc + e[:, i * 128:(i + 1) * 128]
            return acc

        racc[rows, :] = lax.fori_loop(0, N // SB, body, jnp.zeros((R, 128), F32))

    for k in range(Z):
        if k:
            ucs[k - 1].wait_recv()
        score_rows(lax.rem(mz + Z - k, Z))

    def start_rows(it):
        v = jnp.sum(jnp.transpose(racc[...]), axis=0, keepdims=True)
        rsend[it] = v
        out = []
        for k in range(1, Z):
            cp = remote(rsend.at[it], rrecv.at[it, k - 1], rsem_s.at[it, k - 1],
                        rsem_r.at[it, k - 1], proto=zpeer(k))
            cp.start()
            out.append(cp)
        return out

    def end_rows(it, cps):
        for cp in cps:
            cp.wait_recv()
        v = rsend[it]
        for k in range(1, Z):
            v = v + rrecv[it, k - 1]
        return 1.0 / v

    def to_col(v):
        return jnp.transpose(jnp.broadcast_to(v, (128, T)))

    def start_cols(it):
        v = jnp.sum(cs[...], axis=0, keepdims=True)
        CN = N // 16
        colsend[it] = jnp.concatenate([v[:, i * CN:(i + 1) * CN] for i in range(16)],
                                      axis=0).astype(BF16)
        out = []
        for k in range(1, D):
            cp = remote(colsend.at[it], colrecv.at[it, k - 1], csem_s.at[it, k - 1],
                        csem_r.at[it, k - 1], dp=dpeer(k))
            cp.start()
            out.append(cp)
        return out

    def end_cols(it, cps):
        for cp in cps:
            cp.wait_recv()
        v = colsend[it].astype(F32)
        for k in range(1, D):
            v = v + colrecv[it, k - 1].astype(F32)
        v = 1.0 / v
        CN = N // 16
        for i in range(16):
            c8[:, i * CN:(i + 1) * CN] = jnp.broadcast_to(v[i:i + 1, :], (8, CN))

    def row_pass():
        G = 64

        @pl.loop(0, T // G)
        def _(g):
            rows = pl.ds(pl.multiple_of(g * G, G), G)

            def body(j, acc):
                cols = pl.ds(pl.multiple_of(j * 1024, 1024), 1024)
                blk = S.at[rows, cols]
                cblk = c8.at[:, cols]
                for i in range(8):
                    c = cblk[:, i * 128:(i + 1) * 128]
                    new = []
                    for q in range(G // 8):
                        x = blk[q * 8:(q + 1) * 8, i * 128:(i + 1) * 128]
                        new.append(acc[q] + x * x * c)
                    acc = tuple(new)
                return acc

            acc = lax.fori_loop(0, N // 1024, body,
                                tuple(jnp.zeros((8, 128), F32) for _ in range(G // 8)))
            racc[rows, :] = jnp.concatenate(acc, axis=0)

    def col_pass():
        W = 1024

        @pl.loop(0, N // W)
        def _(j):
            def body(g, acc):
                rows = pl.ds(pl.multiple_of(g * 64, 64), 64)
                blk = S.at[rows, pl.ds(pl.multiple_of(j * W, W), W)]
                rblk = rcol.at[rows, :]
                for q in range(8):
                    r = rblk[q * 8:(q + 1) * 8, :]
                    new = []
                    for i in range(W // 128):
                        x = blk[q * 8:(q + 1) * 8, i * 128:(i + 1) * 128]
                        new.append(acc[i] + x * x * r)
                    acc = tuple(new)
                return acc

            acc = lax.fori_loop(0, T // 64, body,
                                tuple(jnp.zeros((8, 128), F32) for _ in range(W // 128)))
            cs[:, pl.ds(pl.multiple_of(j * W, W), W)] = jnp.concatenate(acc, axis=1)

    soft_cps = None
    kf = 1.0 / (SOFT_TEMP * math.sqrt(D * T))
    for it in range(ITERS):
        cps = start_cols(it)
        sends += cps
        if it == 0:
            soft_cps = start_rows(ITERS)
            sends += soft_cps
            ubt[...] = jnp.transpose(ub[...].astype(F32)).astype(BF16)
        end_cols(it, cps)
        row_pass()
        cps = start_rows(it)
        sends += cps
        if it == 0:
            tcol[...] = to_col(end_rows(ITERS, soft_cps) * (PROTOS * kf))
        inv = end_rows(it, cps)
        if it < ITERS - 1:
            rcol[...] = to_col(inv)
            col_pass()
        else:
            rcol[...] = to_col(inv * PROTOS)

    FB = 512
    dacc[...] = jnp.zeros_like(dacc)

    def chunk_cols(q):
        return (pl.ds(q * CW, CW) if q < CHUNKS else pl.ds(N, FI))

    def start_a(q):
        cols = chunk_cols(q)
        cp = remote(gsend.at[pl.ds(pc * H, H), :, cols], garecv.at[:, :, cols],
                    asem_s.at[q], asem_r.at[q], dp=md + 1 - 2 * mc)
        cp.start()
        sends.append(cp)
        return cp

    def start_b(q, cpa):
        cpa.wait_recv()
        cols = chunk_cols(q)

        @pl.loop(0, H)
        def _(k):
            gsend[mc * H + k, :, cols] = (gsend[mc * H + k, :, cols].astype(F32)
                                          + garecv[k, :, cols].astype(F32)).astype(BF16)

        out = []
        for k in range(1, H):
            dst = lax.rem(chip + k, H)
            cp = remote(gsend.at[mc * H + dst, :, cols], gbrecv.at[k - 1, :, cols],
                        bsem_s.at[q, k - 1], bsem_r.at[q, k - 1], dp=dst * 2 + mc)
            cp.start()
            out.append(cp)
        sends.extend(out)
        return out

    def finish(q, cps):
        for cp in cps:
            cp.wait_recv()
        cols = chunk_cols(q)
        v = gsend[mc * H + chip, :, cols].astype(F32)
        for k in range(1, H):
            v = v + gbrecv[k - 1, :, cols].astype(F32)
        if q < CHUNKS:
            pg_ref[:, cols] = v
        else:
            hg_ref[...] = v

    outs = []
    acp = []
    bcp = []
    for q in range(CHUNKS):
        slot = q % 2
        if q >= 2:
            outs[q - 2].wait()

        @pl.loop(0, CW // FB)
        def _(j, q=q, slot=slot):
            lcols = pl.ds(pl.multiple_of(j * FB, FB), FB)
            cols = pl.ds(pl.multiple_of(q * CW + j * FB, FB), FB)
            c = c8[:, cols][0:1, :]

            @pl.loop(0, T // 32)
            def _(g):
                rows = pl.ds(pl.multiple_of(g * 32, 32), 32)
                xv = S.at[rows, cols]
                rv = rcol.at[rows, :]
                tv = tcol.at[rows, :]
                ov = cst.at[slot, rows, lcols]
                dv = dbuf.at[rows, :]
                for h in range(2):
                    hr = slice(h * 16, h * 16 + 16)
                    r = rv[hr, :]
                    t = tv[hr, :]
                    for i in range(FB // 128):
                        hc = slice(i * 128, i * 128 + 128)
                        x = xv[hr, hc]
                        plan = x * x * c[:, hc] * r
                        ov[hr, hc] = plan.astype(BF16)
                        dv[hr, hc] = (x * t - plan * kf).astype(BF16)

            d = dbuf[...]
            dacc[...] += lax.dot_general(d, nb[:, cols], (((1,), (1,)), ((), ())),
                                         preferred_element_type=F32)
            res = jnp.dot(ubt[...], d, preferred_element_type=F32).astype(BF16)
            for e in range(D):
                gsend[(e % 2) * H + e // 2, :, cols] = res[e * ROWS:(e + 1) * ROWS, :]

        cp = pltpu.make_async_copy(cst.at[slot], codes_ref.at[:, pl.ds(q * CW, CW)], osem.at[q])
        cp.start()
        outs.append(cp)
        acp.append(start_a(q))
        if q == CHUNKS - 1:
            for b in range(Z):
                dusend[b] = dacc[b * R:(b + 1) * R, :].astype(BF16)
            dcs = []
            for k in range(1, Z):
                cp = remote(dusend.at[zpeer(k)], durecv.at[k - 1], dsem_s.at[k - 1],
                            dsem_r.at[k - 1], proto=zpeer(k))
                cp.start()
                dcs.append(cp)
            sends += dcs
        if q >= 1:
            bcp.append(start_b(q - 1, acp[q - 1]))

    du = dacc[myrows, :]
    for cp in dcs:
        cp.wait_recv()
    for k in range(1, Z):
        du = du + durecv[k - 1].astype(F32)
    unit = unit_s[...]
    dp = (du - unit * jnp.sum(unit * du, axis=1, keepdims=True)) / len_s[:, 0:1]
    dpall[myrows, :] = dp.astype(BF16)
    hcs = []
    for k in range(1, Z):
        cp = remote(dpall.at[myrows, :], dpall.at[myrows, :], hsem_s.at[k - 1], hsem_r.at[k - 1],
                    proto=zpeer(k))
        cp.start()
        hcs.append(cp)
    sends += hcs
    bcp.append(start_b(CHUNKS - 1, acp[CHUNKS - 1]))
    for cp in hcs:
        cp.wait_recv()
    dpt = jnp.transpose(dpall[...].astype(F32)).astype(BF16)
    res = jnp.dot(dpt, f_ref[...], preferred_element_type=F32).astype(BF16)
    for e in range(D):
        gsend[(e % 2) * H + e // 2, :, N:N + FI] = res[e * ROWS:(e + 1) * ROWS, :]
    acp.append(start_a(CHUNKS))
    finish(0, bcp[0])
    bcp.append(start_b(CHUNKS, acp[CHUNKS]))
    for q in range(1, CHUNKS + 1):
        finish(q, bcp[q])
    for cp in outs[-2:]:
        cp.wait()
    for cp in sends:
        cp.wait_send()


def solution(mesh):
    D, Z = mesh.shape["dp"], mesh.shape["proto"]

    def on_device(features, head_weight, prototypes):
        T, FI = features.shape
        EMB, N = prototypes.shape
        R, H, ROWS, C = T // Z, D // 2, EMB // D, N + FI
        V = pltpu.VMEM
        dma = pltpu.SemaphoreType.DMA
        vspec = pl.BlockSpec(memory_space=pltpu.VMEM)
        return pl.pallas_call(
            functools.partial(kernel, D, Z),
            out_shape=(
                jax.ShapeDtypeStruct((T, N), BF16),
                jax.ShapeDtypeStruct((ROWS, N), F32),
                jax.ShapeDtypeStruct((ROWS, FI), F32),
            ),
            in_specs=[vspec] * 3,
            out_specs=(pl.BlockSpec(memory_space=pl.ANY), vspec, vspec),
            scratch_shapes=[
                V((EMB, N), BF16), V((T, N), F32), V((8, N), F32), V((8, N), F32),
                V((T, 128), F32), V((T, 128), F32), V((T, 128), F32),
                V((Z, R, EMB), BF16), V((Z - 1, R, EMB), BF16),
                V((T, EMB), BF16), V((EMB, T), BF16), V((R, EMB), F32), V((R, 128), F32),
                V((ITERS, 16, N // 16), BF16), V((ITERS, D - 1, 16, N // 16), BF16),
                V((ITERS + 1, 1, T), F32), V((ITERS + 1, Z - 1, 1, T), F32),
                V((2, T, N // CHUNKS), BF16), V((T, 512), BF16), V((T, EMB), F32),
                V((Z, R, EMB), BF16), V((Z - 1, R, EMB), BF16), V((T, EMB), BF16),
                V((D, ROWS, C), BF16), V((H, ROWS, C), BF16), V((H - 1, ROWS, C), BF16),
                dma((Z - 1,)), dma((Z - 1,)), dma((Z - 1,)), dma((Z - 1,)),
                dma((ITERS, D - 1)), dma((ITERS, D - 1)),
                dma((ITERS + 1, Z - 1)), dma((ITERS + 1, Z - 1)),
                dma((Z - 1,)), dma((Z - 1,)), dma((Z - 1,)), dma((Z - 1,)),
                dma((CHUNKS + 1,)), dma((CHUNKS + 1,)),
                dma((CHUNKS + 1, H - 1)), dma((CHUNKS + 1, H - 1)),
                dma((CHUNKS,)),
            ],
            compiler_params=pltpu.CompilerParams(
                collective_id=0, has_side_effects=True, vmem_limit_bytes=60 * 1024 * 1024),
            cost_estimate=pl.CostEstimate(
                flops=6 * T * N * EMB, bytes_accessed=16 * 1024 * 1024,
                transcendentals=T * N),
        )(features, head_weight, prototypes)

    return jax.shard_map(
        on_device, mesh=mesh,
        in_specs=(P("dp", "proto"), P("proto", None), P(None, "proto")),
        out_specs=(P("dp", "proto"), P("dp", "proto"), P("dp", "proto")),
        check_vma=False)
```
